32 devices in a mesh: gx: 16 (over z, y, core), gy: 2 (over x).
Axes of the slice: x: 2, y: 2, z: 4, core: 2. Of those that a mesh axis runs over, the one named last changes fastest.
Arguments:
- source: float32 [64, 128, 256], P('gx', 'gy'), may hold values from -5 to 5
- obstacle: int32 [64, 128, 256], P('gx', 'gy'), may hold values from 0 to 1, as said below
Outputs:
- pressure: float32 [64, 128, 256], P('gx', 'gy')
The draws below stay inside these ranges and needn't reach their ends.
Inputs may be any that keep to these rules, and one draw needn't show every extreme that they name: `obstacle`: 1 marks a cell inside a building, 0 a cell of air.
All inputs are finite; a program needn't handle non-finite values.
Results may differ from the reference program's by a relative error of at most 0.00002.
Values sent between devices are 32-bit elements; how exact they have to be, the bound alone decides.
A program may use at most 64 MiB of HBM per device.

```python
import jax
import jax.numpy as jnp
from jax import lax

NZ = 256
LEVELS = 5
NX = 64
NY = 128


def draw_source(key, part):
    local_key = jax.random.fold_in(key, 11)
    return jnp.clip(jax.random.normal(local_key, (NX, NY, NZ), jnp.float32), -5.0, 5.0)


def draw_obstacle(key, part):
    local_key = jax.random.fold_in(key, 7)
    key_height, key_present = jax.random.split(local_key)
    heights = jax.random.randint(key_height, (NX // 2, NY // 2), 0, NZ // 2 + 1)
    present = jax.random.randint(key_present, (NX // 2, NY // 2), 0, 3)
    heights = jnp.where(present == 0, 0, heights)
    heights = jnp.repeat(jnp.repeat(heights, 2, 0), 2, 1)
    height_axis = lax.iota(jnp.int32, NZ)
    return (height_axis[None, None, :] < heights[:, :, None]).astype(jnp.int32)


def setup_inputs(seed: int = 0) -> dict:
    keys = jax.random.split(jax.random.key(seed), 3)
    return {
        "source": draw_source(jax.random.fold_in(keys[2], 71), 0),
        "obstacle": draw_obstacle(jax.random.fold_in(keys[2], 71), 0),
    }


OMEGA = 0.8
PENALTY = 24.0


def neighbor_sum(padded):
    bordered = jnp.pad(padded, ((0, 0), (0, 0), (1, 1)))
    summed = bordered[2:, 1:-1, 1:-1] + bordered[:-2, 1:-1, 1:-1]
    summed = summed + bordered[1:-1, 2:, 1:-1] + bordered[1:-1, :-2, 1:-1]
    summed = summed + bordered[1:-1, 1:-1, 2:] + bordered[1:-1, 1:-1, :-2]
    return summed


def restrict(residual):
    size_x, size_y, size_z = residual.shape
    blocks = residual.reshape(size_x // 2, 2, size_y // 2, 2, size_z // 2, 2)
    return blocks.sum(axis=(1, 3, 5)) * 0.125


def prolong(correction):
    return jnp.repeat(jnp.repeat(jnp.repeat(correction, 2, 0), 2, 1), 2, 2)


def plane_pad(field):
    return jnp.pad(field, ((1, 1), (1, 1), (0, 0)))


def reference(source, obstacle):
    solid_cells = obstacle.astype(jnp.float32)
    source_fluid = (1.0 - solid_cells) * source
    diagonal = 6.0 + PENALTY * solid_cells
    weight = OMEGA / diagonal

    def operator(field, grid_level):
        if grid_level == 0:
            return diagonal * field - neighbor_sum(plane_pad(field))
        return (6.0 * field - neighbor_sum(plane_pad(field))) * (0.25 ** grid_level)

    def cycle(residual, grid_level):
        if grid_level == 0:
            damping = weight
        else:
            damping = OMEGA / (6.0 * 0.25 ** grid_level)
        correction = damping * residual
        if grid_level == LEVELS - 1:
            return correction + damping * (residual - operator(correction, grid_level))
        leftover = residual - operator(correction, grid_level)
        correction = correction + prolong(cycle(restrict(leftover), grid_level + 1))
        return correction + damping * (residual - operator(correction, grid_level))

    return cycle(source_fluid, 0)
```

```python
import functools

import jax
import jax.numpy as jnp
from jax import lax
from jax.experimental import pallas as pl
from jax.experimental.pallas import tpu as pltpu
from jax.sharding import PartitionSpec as P

C = 0.8 / 6.0
CS = 0.8 / 30.0
D1, D2, D3, D4 = C * 4.0, C * 16.0, C * 64.0, C * 256.0
MESH = pl.DeviceIdType.MESH
F32 = jnp.float32
BF16 = jnp.bfloat16


def roll(a, by, axis):
    return pltpu.roll(a, by % a.shape[axis], axis)


def pair_matrix(rows, cols, used_rows, used_cols, down):
    k = lax.broadcasted_iota(jnp.int32, (rows, cols), 0)
    j = lax.broadcasted_iota(jnp.int32, (rows, cols), 1)
    hit = (k // 2 == j) if down else (j // 2 == k)
    hit = hit & (k < used_rows) & (j < used_cols)
    return jnp.where(hit, 1.0, 0.0).astype(BF16)


def split_dot(x, matrix):
    hi = x.astype(BF16)
    rest = x - hi.astype(F32)
    mid = rest.astype(BF16)
    lo = (rest - mid.astype(F32)).astype(BF16)
    out = jnp.dot(hi, matrix, preferred_element_type=F32)
    out = out + jnp.dot(mid, matrix, preferred_element_type=F32)
    return out + jnp.dot(lo, matrix, preferred_element_type=F32)


def z_sum(a, full):
    left, right = roll(a, 1, 1), roll(a, -1, 1)
    if full:
        lane = lax.broadcasted_iota(jnp.int32, a.shape, 1)
        left = jnp.where(lane == 0, 0.0, left)
        right = jnp.where(lane == a.shape[1] - 1, 0.0, right)
    return left + right


def neighbors(a, planes, rows, full, mask_y=True):
    up, down = roll(a, 1, 0), roll(a, -1, 0)
    if mask_y:
        y = lax.broadcasted_iota(jnp.int32, a.shape, 0) % rows
        up = jnp.where(y == 0, 0.0, up)
        down = jnp.where(y == rows - 1, 0.0, down)
    zero = jnp.zeros((rows, a.shape[1]), F32)
    below = jnp.concatenate([zero, a[: (planes - 1) * rows]], 0)
    above = jnp.concatenate([a[rows:], zero], 0)
    return below + above + up + down + z_sum(a, full)


def x_pairs(a, planes, rows):
    return jnp.concatenate(
        [
            a[2 * i * rows : (2 * i + 1) * rows] + a[(2 * i + 1) * rows : (2 * i + 2) * rows]
            for i in range(planes // 2)
        ],
        0,
    )


def kernel(
    n, m, source_ref, obstacle_ref, out_ref,
    sf_ref, xh, yh, ys, r1, gathered, packed, a2, e3s, q2, e2s, e21, e1s, tmp,
    send, recv, gsend, grecv,
):
    gx, gy = lax.axis_index("gx"), lax.axis_index("gy")
    windowed = n > 16
    window = 28 if windowed else 16
    yrows = 16 * m

    def base_of(x):
        return 4 * (x // 4) - 12 if windowed else 0

    base = base_of(gx)

    def peers(fn):
        if not windowed:
            flat = gx * m + gy
            for k in range(1, n * m):
                other = lax.rem(flat + k, n * m)
                fn(other // m, lax.rem(other, m))
            return

        def step(k, carry):
            x, y = base + k // m, lax.rem(k, m)

            @pl.when((x >= 0) & (x < n) & ((x != gx) | (y != gy)))
            def _():
                fn(x, y)

            return carry

        lax.fori_loop(0, window * m, step, 0)

    def exists(dx, dy):
        x, y = gx + dx, gy + dy
        return (x >= 0) & (x < n) & (y >= 0) & (y < m)

    def halo(k, src, dst, dx, dy):
        copy = pltpu.make_async_remote_copy(
            src_ref=src,
            dst_ref=dst,
            send_sem=send.at[k],
            recv_sem=recv.at[k],
            device_id=(jnp.clip(gx + dx, 0, n - 1), jnp.clip(gy + dy, 0, m - 1)),
            device_id_type=MESH,
        )

        def start():
            pl.when(exists(dx, dy))(lambda: copy.start())

        def wait_recv():
            pl.when(exists(-dx, -dy))(lambda: copy.wait_recv())

        def wait_send():
            pl.when(exists(dx, dy))(lambda: copy.wait_send())

        return start, wait_recv, wait_send

    xh[...] = jnp.zeros_like(xh)
    yh[...] = jnp.zeros_like(yh)
    r1[...] = jnp.zeros_like(r1)
    if windowed:
        gathered[...] = jnp.zeros_like(gathered)
    barrier = pltpu.get_barrier_semaphore()

    def greet(x, y):
        pl.semaphore_signal(barrier, inc=1, device_id=(x, y), device_id_type=MESH)

    peers(greet)

    ys[...] = jnp.zeros_like(ys)
    for i in range(4):
        plane = jnp.where(obstacle_ref[i] == 0, source_ref[i], 0.0)
        sf_ref[i] = plane
        ys[0, i : i + 1, :] = plane[0:1]
        ys[1, i : i + 1, :] = plane[63:64]
    e3s[...] = jnp.zeros_like(e3s)
    e2s[...] = jnp.zeros_like(e2s)
    a2[...] = jnp.zeros_like(a2)

    if not windowed:
        pl.semaphore_wait(barrier, n * m - 1)
    else:
        peers(lambda x, y: pl.semaphore_wait(barrier, 1))

    halos = []

    def add(src, dst, dx, dy):
        halos.append(halo(len(halos), src, dst, dx, dy))
        return halos[-1]

    first = [
        add(sf_ref.at[3], xh.at[0], 1, 0),
        add(sf_ref.at[0], xh.at[1], -1, 0),
        add(ys.at[1], yh.at[0], 0, 1),
        add(ys.at[0], yh.at[1], 0, -1),
    ]
    for start, _, _ in first:
        start()

    row = lax.broadcasted_iota(jnp.int32, (64, 256), 0)

    def fine_neighbors(planes, i, above_row, below_row):
        p = planes[i + 1]
        up = jnp.where(row == 0, above_row, roll(p, 1, 0))
        down = jnp.where(row == 63, below_row, roll(p, -1, 0))
        return planes[i] + planes[i + 2] + up + down + z_sum(p, True)

    for _, wait, _ in first:
        wait()
    planes = [xh[0]] + [sf_ref[i] for i in range(4)] + [xh[1]]
    left = [
        0.2 * planes[i + 1]
        + C * fine_neighbors(planes, i, yh[0, i : i + 1, :], yh[1, i : i + 1, :])
        for i in range(4)
    ]
    summed = jnp.concatenate([left[0] + left[1], left[2] + left[3]], 0)
    tmp[0:128] = split_dot(summed, pair_matrix(256, 128, 256, 128, True)) * 0.125
    for i in range(2):
        own = tmp[pl.ds(64 * i, 32, stride=2), :] + tmp[pl.ds(64 * i + 1, 32, stride=2), :]
        r1[2 + i, 8:40, :] = own

    mid = pl.ds(8, 32)
    second = [
        add(r1.at[3, mid], r1.at[1, mid], 1, 0),
        add(r1.at[2, mid], r1.at[4, mid], -1, 0),
        add(r1.at[pl.ds(2, 2), pl.ds(32, 8)], r1.at[pl.ds(2, 2), pl.ds(0, 8)], 0, 1),
        add(r1.at[pl.ds(2, 2), pl.ds(8, 8)], r1.at[pl.ds(2, 2), pl.ds(40, 8)], 0, -1),
    ]
    third = [
        add(r1.at[2, mid], r1.at[0, mid], 1, 0),
        add(r1.at[3, mid], r1.at[5, mid], -1, 0),
        add(r1.at[3, pl.ds(32, 8)], r1.at[1, pl.ds(0, 8)], 1, 1),
        add(r1.at[3, pl.ds(8, 8)], r1.at[1, pl.ds(40, 8)], 1, -1),
        add(r1.at[2, pl.ds(32, 8)], r1.at[4, pl.ds(0, 8)], -1, 1),
        add(r1.at[2, pl.ds(8, 8)], r1.at[4, pl.ds(40, 8)], -1, -1),
    ]
    for start, _, _ in second + third:
        start()
    for _, wait, _ in second:
        wait()

    near = [r1[k, 8:40, :] for k in range(1, 5)]
    left1 = []
    for i in (1, 2):
        p = r1[i + 1]
        total = (roll(p, 1, 0) + roll(p, -1, 0) + z_sum(p, True))[8:40]
        left1.append(0.2 * near[i] + C * (near[i - 1] + near[i + 1] + total))
    tmp[0:32] = split_dot(left1[0] + left1[1], pair_matrix(128, 128, 128, 64, True)) * 0.125
    r2 = tmp[pl.ds(0, 16, stride=2), :] + tmp[pl.ds(1, 16, stride=2), :]
    mine = r2[0:8] + roll(r2[8:16], 64, 1)
    packed[...] = mine
    gathered[(gx - base) * m + gy] = mine

    def tile_copy(x, y):
        return pltpu.make_async_remote_copy(
            src_ref=packed,
            dst_ref=gathered.at[(gx - base_of(x)) * m + gy],
            send_sem=gsend,
            recv_sem=grecv,
            device_id=(x, y),
            device_id_type=MESH,
        )

    peers(lambda x, y: tile_copy(x, y).start())
    if not windowed:
        many = gathered.at[pl.ds(0, n * m - 1)]
        pltpu.make_async_copy(many, many, grecv).wait()
    else:
        peers(lambda x, y: tile_copy(x, y).wait_recv())

    def inside(a, planes, rows, first_plane, count):
        if not windowed:
            return a
        x = first_plane + lax.broadcasted_iota(jnp.int32, a.shape, 0) // rows
        return jnp.where((x >= 0) & (x < count), a, 0.0)

    tiles = gathered[...].reshape(window * m * 8, 128)
    lane = lax.broadcasted_iota(jnp.int32, tiles.shape, 1)
    low = jnp.where(lane < 64, tiles, 0.0).reshape(window * m, 8, 128)
    high = jnp.where(lane < 64, roll(tiles, 64, 1), 0.0).reshape(window * m, 8, 128)
    a2[pl.ds(2 * m, window * m), 0:8, :] = low
    a2[pl.ds(2 * m, window * m), 8:16, :] = high
    full2 = a2[pl.ds(2 * m, window * m)].reshape(window * yrows, 128)

    def restrict(a, planes, rows, used):
        count = planes // 2 * rows
        folded = x_pairs(a, planes, rows)
        tmp[0:count] = split_dot(folded, pair_matrix(128, 128, used, used // 2, True)) * 0.125
        half = count // 2
        return tmp[pl.ds(0, half, stride=2), :] + tmp[pl.ds(1, half, stride=2), :]

    def prolong_yz(a, used, dst):
        wide = split_dot(a, pair_matrix(128, 128, used, used * 2, False))
        dst[pl.ds(0, a.shape[0], stride=2), :] = wide
        dst[pl.ds(1, a.shape[0], stride=2), :] = wide

    x3, y3 = window // 2, yrows // 2
    x4, y4 = window // 4, yrows // 4
    r3 = restrict(0.2 * full2 + C * neighbors(full2, window, yrows, False), window, yrows, 64)
    r4 = restrict(0.2 * r3 + C * neighbors(r3, x3, y3, False), x3, y3, 32)
    e4 = D4 * (1.2 * r4 + C * neighbors(r4, x4, y4, False))
    e4 = inside(e4, x4, y4, base // 4, n // 4)
    prolong_yz(e4, 16, tmp)
    e3 = D3 * r3 + jnp.concatenate(
        [tmp[pl.ds((i // 2) * y3, y3), :] for i in range(x3)], 0
    )
    e3 = 0.2 * e3 + D3 * r3 + C * neighbors(e3, x3, y3, False)
    e3 = inside(e3, x3, y3, base // 2, n // 2)
    e3s[pl.ds(1, x3)] = e3.reshape(x3, y3, 128)

    low3 = (gx - base + 2) // 2 - 1
    prolong_yz(e3s[pl.ds(low3, 3)].reshape(3 * y3, 128), 32, q2)
    odd = lax.rem(gx, 2)
    rs, es = [], []
    for d in range(-2, 3):
        plane = a2[pl.ds((gx - base + 2 + d) * m, m)].reshape(yrows, 128)
        start = pl.multiple_of(((odd + d + 2) // 2) * yrows, 8)
        rs.append(plane)
        es.append(D2 * plane + q2[pl.ds(start, yrows), :])
    rs, es = jnp.concatenate(rs, 0), jnp.concatenate(es, 0)
    e2 = 0.2 * es + D2 * rs + C * neighbors(es, 5, yrows, False)
    e2 = e2[yrows : 4 * yrows]
    wide = split_dot(e2, pair_matrix(128, 128, 64, 128, False))
    alive = [jnp.where(gx > 0, 1.0, 0.0), 1.0, jnp.where(gx < n - 1, 1.0, 0.0)]
    for i in range(3):
        e2s[i, pl.ds(8, yrows), :] = wide[i * yrows : (i + 1) * yrows] * alive[i]
    for i in range(3):
        part = e2s[i, pl.ds(gy * 16 + 4, 24), :]
        e21[pl.ds(48 * i, 24, stride=2), :] = part
        e21[pl.ds(48 * i + 1, 24, stride=2), :] = part

    for _, wait, _ in third:
        wait()
    r1s = [r1[k] for k in range(6)]
    e1p = [D1 * r1s[k] + e21[48 * (k // 2) : 48 * (k // 2) + 48, :] for k in range(6)]
    y = gy * 32 - 8 + lax.broadcasted_iota(jnp.int32, (48, 128), 0)
    y_in = (y >= 0) & (y < 32 * m)
    done = []
    for k in range(1, 5):
        p = e1p[k]
        total = e1p[k - 1] + e1p[k + 1] + roll(p, 1, 0) + roll(p, -1, 0) + z_sum(p, True)
        value = jnp.where(y_in, 0.2 * p + D1 * r1s[k] + C * total, 0.0)
        if k == 1:
            value = value * alive[0]
        if k == 4:
            value = value * alive[2]
        done.append(value)
    done = jnp.concatenate(done, 0)
    wide = split_dot(done, pair_matrix(128, 256, 128, 256, False))
    for h in range(2):
        half = wide[:, 128 * h : 128 * h + 128]
        e1s[h, pl.ds(0, 192, stride=2), :] = half
        e1s[h, pl.ds(1, 192, stride=2), :] = half

    def coarse(k, start, rows):
        return jnp.concatenate([e1s[h, 96 * k + start : 96 * k + start + rows, :] for h in (0, 1)], 1)

    blocks = [coarse(k, 16, 64) for k in range(4)]
    planes = [C * xh[0] + blocks[0]]
    planes += [C * sf_ref[i] + blocks[1 + i // 2] for i in range(4)]
    planes += [C * xh[1] + blocks[3]]
    for i in range(4):
        k = 1 + i // 2
        above = C * yh[0, i : i + 1, :] + coarse(k, 15, 1)
        below = C * yh[1, i : i + 1, :] + coarse(k, 80, 1)
        total = fine_neighbors(planes, i, above, below)
        weight = jnp.where(obstacle_ref[i] == 0, C, CS)
        out_ref[i] = 0.2 * planes[i + 1] + weight * (sf_ref[i] + total)

    for _, _, wait in halos:
        wait()
    if not windowed:
        many = gathered.at[pl.ds(0, n * m - 1)]
        pltpu.make_async_copy(many, many, gsend).wait()
    else:
        peers(lambda x, y: tile_copy(x, y).wait_send())


def solution(mesh):
    n, m = mesh.shape["gx"], mesh.shape["gy"]
    window = 28 if n > 16 else 16
    rows = 16 * m

    def body(source, obstacle):
        vmem = pl.BlockSpec(memory_space=pltpu.VMEM)
        return pl.pallas_call(
            functools.partial(kernel, n, m),
            out_shape=jax.ShapeDtypeStruct(source.shape, F32),
            in_specs=[vmem, vmem],
            out_specs=vmem,
            scratch_shapes=[
                pltpu.VMEM((4, 64, 256), F32),
                pltpu.VMEM((2, 64, 256), F32),
                pltpu.VMEM((2, 8, 256), F32),
                pltpu.VMEM((2, 8, 256), F32),
                pltpu.VMEM((6, 48, 128), F32),
                pltpu.VMEM((window * m, 8, 128), F32),
                pltpu.VMEM((8, 128), F32),
                pltpu.VMEM(((window + 4) * m, 16, 128), F32),
                pltpu.VMEM((window // 2 + 2, rows // 2, 128), F32),
                pltpu.VMEM((3 * rows, 128), F32),
                pltpu.VMEM((3, rows + 16, 128), F32),
                pltpu.VMEM((144, 128), F32),
                pltpu.VMEM((2, 384, 128), F32),
                pltpu.VMEM((max(128, window // 2 * rows), 128), F32),
                pltpu.SemaphoreType.DMA((14,)),
                pltpu.SemaphoreType.DMA((14,)),
                pltpu.SemaphoreType.DMA,
                pltpu.SemaphoreType.DMA,
            ],
            compiler_params=pltpu.CompilerParams(
                collective_id=0, has_side_effects=True, vmem_limit_bytes=32 * 1024 * 1024
            ),
        )(source, obstacle)

    spec = P("gx", "gy", None)
    return jax.shard_map(
        body, mesh=mesh, in_specs=(spec, spec), out_specs=spec, check_vma=False
    )
```

```python
import functools

import jax
import jax.numpy as jnp
from jax import lax
from jax.experimental import pallas as pl
from jax.experimental.pallas import tpu as pltpu
from jax.sharding import PartitionSpec as P

C = 0.8 / 6.0
CS = 0.8 / 30.0
D1, D2, D3, D4 = C * 4.0, C * 16.0, C * 64.0, C * 256.0
MESH = pl.DeviceIdType.MESH
F32 = jnp.float32
BF16 = jnp.bfloat16


def roll(a, by, axis):
    return pltpu.roll(a, by % a.shape[axis], axis)


def pair_matrix(rows, cols, used_rows, used_cols, down):
    k = lax.broadcasted_iota(jnp.int32, (rows, cols), 0)
    j = lax.broadcasted_iota(jnp.int32, (rows, cols), 1)
    hit = (k // 2 == j) if down else (j // 2 == k)
    hit = hit & (k < used_rows) & (j < used_cols)
    return jnp.where(hit, 1.0, 0.0).astype(BF16)


def split_dot(x, matrix):
    hi = x.astype(BF16)
    rest = x - hi.astype(F32)
    mid = rest.astype(BF16)
    lo = (rest - mid.astype(F32)).astype(BF16)
    out = jnp.dot(hi, matrix, preferred_element_type=F32)
    out = out + jnp.dot(mid, matrix, preferred_element_type=F32)
    return out + jnp.dot(lo, matrix, preferred_element_type=F32)


def z_sum(a, full):
    left, right = roll(a, 1, 1), roll(a, -1, 1)
    if full:
        lane = lax.broadcasted_iota(jnp.int32, a.shape, 1)
        left = jnp.where(lane == 0, 0.0, left)
        right = jnp.where(lane == a.shape[1] - 1, 0.0, right)
    return left + right


def neighbors(a, planes, rows, full, mask_y=True):
    up, down = roll(a, 1, 0), roll(a, -1, 0)
    if mask_y:
        y = lax.broadcasted_iota(jnp.int32, a.shape, 0)
        y = y & (rows - 1) if rows & (rows - 1) == 0 else y % rows
        up = jnp.where(y == 0, 0.0, up)
        down = jnp.where(y == rows - 1, 0.0, down)
    zero = jnp.zeros((rows, a.shape[1]), F32)
    below = jnp.concatenate([zero, a[: (planes - 1) * rows]], 0)
    above = jnp.concatenate([a[rows:], zero], 0)
    return below + above + up + down + z_sum(a, full)


def x_pairs(a, planes, rows):
    return jnp.concatenate(
        [
            a[2 * i * rows : (2 * i + 1) * rows] + a[(2 * i + 1) * rows : (2 * i + 2) * rows]
            for i in range(planes // 2)
        ],
        0,
    )


def kernel(
    n, m, source_ref, obstacle_ref, out_ref,
    src, obs, sf_ref, xh, yh, ys, r1, gathered, packed, a2, e3s, q2, e2s, e21, e1s, tmp,
    send, recv, gsend, grecv, load,
):
    gx, gy = lax.axis_index("gx"), lax.axis_index("gy")
    windowed = n > 16
    window = 28 if windowed else 16
    yrows = 16 * m

    def base_of(x):
        return 4 * (x // 4) - 12 if windowed else 0

    base = base_of(gx)

    def peers(fn):
        if not windowed:
            flat = gx * m + gy
            for k in range(1, n * m):
                other = lax.rem(flat + k, n * m)
                fn(other // m, lax.rem(other, m))
            return

        def step(k, carry):
            x, y = base + k // m, lax.rem(k, m)

            @pl.when((x >= 0) & (x < n) & ((x != gx) | (y != gy)))
            def _():
                fn(x, y)

            return carry

        lax.fori_loop(0, window * m, step, 0)

    def exists(dx, dy):
        x, y = gx + dx, gy + dy
        return (x >= 0) & (x < n) & (y >= 0) & (y < m)

    def halo(k, src, dst, dx, dy):
        copy = pltpu.make_async_remote_copy(
            src_ref=src,
            dst_ref=dst,
            send_sem=send.at[k],
            recv_sem=recv.at[k],
            device_id=(jnp.clip(gx + dx, 0, n - 1), jnp.clip(gy + dy, 0, m - 1)),
            device_id_type=MESH,
        )

        def start():
            pl.when(exists(dx, dy))(lambda: copy.start())

        def wait_recv():
            pl.when(exists(-dx, -dy))(lambda: copy.wait_recv())

        def wait_send():
            pl.when(exists(dx, dy))(lambda: copy.wait_send())

        return start, wait_recv, wait_send

    loads = [
        pltpu.make_async_copy(source_ref, src, load.at[0]),
        pltpu.make_async_copy(obstacle_ref, obs, load.at[1]),
    ]
    for copy in loads:
        copy.start()
    xh[...] = jnp.zeros_like(xh)
    yh[...] = jnp.zeros_like(yh)
    r1[...] = jnp.zeros_like(r1)
    if windowed:
        gathered[...] = jnp.zeros_like(gathered)
    barrier = pltpu.get_barrier_semaphore()

    def greet(x, y):
        pl.semaphore_signal(barrier, inc=1, device_id=(x, y), device_id_type=MESH)

    peers(greet)

    ys[...] = jnp.zeros_like(ys)
    e3s[...] = jnp.zeros_like(e3s)
    e2s[...] = jnp.zeros_like(e2s)
    a2[...] = jnp.zeros_like(a2)
    for copy in loads:
        copy.wait()
    for i in range(4):
        plane = jnp.where(obs[i] == 0, src[i], 0.0)
        sf_ref[i] = plane
        ys[0, i : i + 1, :] = plane[0:1]
        ys[1, i : i + 1, :] = plane[63:64]

    if not windowed:
        pl.semaphore_wait(barrier, n * m - 1)
    else:
        peers(lambda x, y: pl.semaphore_wait(barrier, 1))

    halos = []

    def add(src, dst, dx, dy):
        halos.append(halo(len(halos), src, dst, dx, dy))
        return halos[-1]

    first = [
        add(sf_ref.at[3], xh.at[0], 1, 0),
        add(sf_ref.at[0], xh.at[1], -1, 0),
        add(ys.at[1], yh.at[0], 0, 1),
        add(ys.at[0], yh.at[1], 0, -1),
    ]
    for start, _, _ in first:
        start()

    row = lax.broadcasted_iota(jnp.int32, (64, 256), 0)

    def fine_neighbors(planes, i, above_row, below_row):
        p = planes[i + 1]
        up = jnp.where(row == 0, above_row, roll(p, 1, 0))
        down = jnp.where(row == 63, below_row, roll(p, -1, 0))
        return planes[i] + planes[i + 2] + up + down + z_sum(p, True)

    for _, wait, _ in first:
        wait()
    planes = [xh[0]] + [sf_ref[i] for i in range(4)] + [xh[1]]
    left = [
        0.2 * planes[i + 1]
        + C * fine_neighbors(planes, i, yh[0, i : i + 1, :], yh[1, i : i + 1, :])
        for i in range(4)
    ]
    summed = jnp.concatenate([left[0] + left[1], left[2] + left[3]], 0)
    tmp[0:128] = split_dot(summed, pair_matrix(256, 128, 256, 128, True)) * 0.125
    for i in range(2):
        own = tmp[pl.ds(64 * i, 32, stride=2), :] + tmp[pl.ds(64 * i + 1, 32, stride=2), :]
        r1[2 + i, 8:40, :] = own

    mid = pl.ds(8, 32)
    second = [
        add(r1.at[3, mid], r1.at[1, mid], 1, 0),
        add(r1.at[2, mid], r1.at[4, mid], -1, 0),
        add(r1.at[pl.ds(2, 2), pl.ds(32, 8)], r1.at[pl.ds(2, 2), pl.ds(0, 8)], 0, 1),
        add(r1.at[pl.ds(2, 2), pl.ds(8, 8)], r1.at[pl.ds(2, 2), pl.ds(40, 8)], 0, -1),
    ]
    third = [
        add(r1.at[2, mid], r1.at[0, mid], 1, 0),
        add(r1.at[3, mid], r1.at[5, mid], -1, 0),
        add(r1.at[3, pl.ds(32, 8)], r1.at[1, pl.ds(0, 8)], 1, 1),
        add(r1.at[3, pl.ds(8, 8)], r1.at[1, pl.ds(40, 8)], 1, -1),
        add(r1.at[2, pl.ds(32, 8)], r1.at[4, pl.ds(0, 8)], -1, 1),
        add(r1.at[2, pl.ds(8, 8)], r1.at[4, pl.ds(40, 8)], -1, -1),
    ]
    for start, _, _ in second + third:
        start()
    for _, wait, _ in second:
        wait()

    near = [r1[k, 8:40, :] for k in range(1, 5)]
    left1 = []
    for i in (1, 2):
        p = r1[i + 1]
        total = (roll(p, 1, 0) + roll(p, -1, 0) + z_sum(p, True))[8:40]
        left1.append(0.2 * near[i] + C * (near[i - 1] + near[i + 1] + total))
    tmp[0:32] = split_dot(left1[0] + left1[1], pair_matrix(128, 128, 128, 64, True)) * 0.125
    r2 = tmp[pl.ds(0, 16, stride=2), :] + tmp[pl.ds(1, 16, stride=2), :]
    mine = r2[0:8] + roll(r2[8:16], 64, 1)
    packed[...] = mine
    gathered[(gx - base) * m + gy] = mine

    def tile_copy(x, y):
        return pltpu.make_async_remote_copy(
            src_ref=packed,
            dst_ref=gathered.at[(gx - base_of(x)) * m + gy],
            send_sem=gsend,
            recv_sem=grecv,
            device_id=(x, y),
            device_id_type=MESH,
        )

    peers(lambda x, y: tile_copy(x, y).start())
    if not windowed:
        many = gathered.at[pl.ds(0, n * m - 1)]
        pltpu.make_async_copy(many, many, grecv).wait()
    else:
        peers(lambda x, y: tile_copy(x, y).wait_recv())

    def inside(a, planes, rows, first_plane, count):
        if not windowed:
            return a
        x = first_plane + lax.broadcasted_iota(jnp.int32, a.shape, 0) // rows
        return jnp.where((x >= 0) & (x < count), a, 0.0)

    tiles = gathered[...].reshape(window * m * 8, 128)
    lane = lax.broadcasted_iota(jnp.int32, tiles.shape, 1)
    low = jnp.where(lane < 64, tiles, 0.0).reshape(window * m, 8, 128)
    high = jnp.where(lane < 64, roll(tiles, 64, 1), 0.0).reshape(window * m, 8, 128)
    a2[pl.ds(2 * m, window * m), 0:8, :] = low
    a2[pl.ds(2 * m, window * m), 8:16, :] = high
    full2 = a2[pl.ds(2 * m, window * m)].reshape(window * yrows, 128)

    def restrict(a, planes, rows, used):
        count = planes // 2 * rows
        folded = x_pairs(a, planes, rows)
        tmp[0:count] = split_dot(folded, pair_matrix(128, 128, used, used // 2, True)) * 0.125
        half = count // 2
        return tmp[pl.ds(0, half, stride=2), :] + tmp[pl.ds(1, half, stride=2), :]

    def prolong_yz(a, used, dst):
        wide = split_dot(a, pair_matrix(128, 128, used, used * 2, False))
        dst[pl.ds(0, a.shape[0], stride=2), :] = wide
        dst[pl.ds(1, a.shape[0], stride=2), :] = wide

    x3, y3 = window // 2, yrows // 2
    x4, y4 = window // 4, yrows // 4
    r3 = restrict(0.2 * full2 + C * neighbors(full2, window, yrows, False), window, yrows, 64)
    r4 = restrict(0.2 * r3 + C * neighbors(r3, x3, y3, False), x3, y3, 32)
    e4 = D4 * (1.2 * r4 + C * neighbors(r4, x4, y4, False))
    e4 = inside(e4, x4, y4, base // 4, n // 4)
    prolong_yz(e4, 16, tmp)
    e3 = D3 * r3 + jnp.concatenate(
        [tmp[pl.ds((i // 2) * y3, y3), :] for i in range(x3)], 0
    )
    e3 = 0.2 * e3 + D3 * r3 + C * neighbors(e3, x3, y3, False)
    e3 = inside(e3, x3, y3, base // 2, n // 2)
    e3s[pl.ds(1, x3)] = e3.reshape(x3, y3, 128)

    low3 = (gx - base + 2) // 2 - 1
    prolong_yz(e3s[pl.ds(low3, 3)].reshape(3 * y3, 128), 32, q2)
    odd = lax.rem(gx, 2)
    rs, es = [], []
    for d in range(-2, 3):
        plane = a2[pl.ds((gx - base + 2 + d) * m, m)].reshape(yrows, 128)
        start = pl.multiple_of(((odd + d + 2) // 2) * yrows, 8)
        rs.append(plane)
        es.append(D2 * plane + q2[pl.ds(start, yrows), :])
    rs, es = jnp.concatenate(rs, 0), jnp.concatenate(es, 0)
    e2 = 0.2 * es + D2 * rs + C * neighbors(es, 5, yrows, False)
    e2 = e2[yrows : 4 * yrows]
    wide = split_dot(e2, pair_matrix(128, 128, 64, 128, False))
    alive = [jnp.where(gx > 0, 1.0, 0.0), 1.0, jnp.where(gx < n - 1, 1.0, 0.0)]
    for i in range(3):
        e2s[i, pl.ds(8, yrows), :] = wide[i * yrows : (i + 1) * yrows] * alive[i]
    for i in range(3):
        part = e2s[i, pl.ds(gy * 16 + 4, 24), :]
        e21[pl.ds(48 * i, 24, stride=2), :] = part
        e21[pl.ds(48 * i + 1, 24, stride=2), :] = part

    for _, wait, _ in third:
        wait()
    r1s = [r1[k] for k in range(6)]
    e1p = [D1 * r1s[k] + e21[48 * (k // 2) : 48 * (k // 2) + 48, :] for k in range(6)]
    y = gy * 32 - 8 + lax.broadcasted_iota(jnp.int32, (48, 128), 0)
    y_in = (y >= 0) & (y < 32 * m)
    done = []
    for k in range(1, 5):
        p = e1p[k]
        total = e1p[k - 1] + e1p[k + 1] + roll(p, 1, 0) + roll(p, -1, 0) + z_sum(p, True)
        value = jnp.where(y_in, 0.2 * p + D1 * r1s[k] + C * total, 0.0)
        if k == 1:
            value = value * alive[0]
        if k == 4:
            value = value * alive[2]
        done.append(value)
    done = jnp.concatenate(done, 0)
    wide = split_dot(done, pair_matrix(128, 256, 128, 256, False))
    for h in range(2):
        half = wide[:, 128 * h : 128 * h + 128]
        e1s[h, pl.ds(0, 192, stride=2), :] = half
        e1s[h, pl.ds(1, 192, stride=2), :] = half

    def coarse(k, start, rows):
        return jnp.concatenate([e1s[h, 96 * k + start : 96 * k + start + rows, :] for h in (0, 1)], 1)

    blocks = [coarse(k, 16, 64) for k in range(4)]
    planes = [C * xh[0] + blocks[0]]
    planes += [C * sf_ref[i] + blocks[1 + i // 2] for i in range(4)]
    planes += [C * xh[1] + blocks[3]]
    for i in range(4):
        k = 1 + i // 2
        above = C * yh[0, i : i + 1, :] + coarse(k, 15, 1)
        below = C * yh[1, i : i + 1, :] + coarse(k, 80, 1)
        total = fine_neighbors(planes, i, above, below)
        weight = jnp.where(obs[i] == 0, C, CS)
        out_ref[i] = 0.2 * planes[i + 1] + weight * (sf_ref[i] + total)

    for _, _, wait in halos:
        wait()
    if not windowed:
        many = gathered.at[pl.ds(0, n * m - 1)]
        pltpu.make_async_copy(many, many, gsend).wait()
    else:
        peers(lambda x, y: tile_copy(x, y).wait_send())


def solution(mesh):
    n, m = mesh.shape["gx"], mesh.shape["gy"]
    window = 28 if n > 16 else 16
    rows = 16 * m

    def body(source, obstacle):
        vmem = pl.BlockSpec(memory_space=pltpu.VMEM)
        return pl.pallas_call(
            functools.partial(kernel, n, m),
            out_shape=jax.ShapeDtypeStruct(source.shape, F32),
            in_specs=[pl.BlockSpec(memory_space=pltpu.HBM)] * 2,
            out_specs=vmem,
            scratch_shapes=[
                pltpu.VMEM(source.shape, F32),
                pltpu.VMEM(source.shape, jnp.int32),
                pltpu.VMEM((4, 64, 256), F32),
                pltpu.VMEM((2, 64, 256), F32),
                pltpu.VMEM((2, 8, 256), F32),
                pltpu.VMEM((2, 8, 256), F32),
                pltpu.VMEM((6, 48, 128), F32),
                pltpu.VMEM((window * m, 8, 128), F32),
                pltpu.VMEM((8, 128), F32),
                pltpu.VMEM(((window + 4) * m, 16, 128), F32),
                pltpu.VMEM((window // 2 + 2, rows // 2, 128), F32),
                pltpu.VMEM((3 * rows, 128), F32),
                pltpu.VMEM((3, rows + 16, 128), F32),
                pltpu.VMEM((144, 128), F32),
                pltpu.VMEM((2, 384, 128), F32),
                pltpu.VMEM((max(128, window // 2 * rows), 128), F32),
                pltpu.SemaphoreType.DMA((14,)),
                pltpu.SemaphoreType.DMA((14,)),
                pltpu.SemaphoreType.DMA,
                pltpu.SemaphoreType.DMA,
                pltpu.SemaphoreType.DMA((2,)),
            ],
            compiler_params=pltpu.CompilerParams(
                collective_id=0, has_side_effects=True, vmem_limit_bytes=32 * 1024 * 1024
            ),
        )(source, obstacle)

    spec = P("gx", "gy", None)
    return jax.shard_map(
        body, mesh=mesh, in_specs=(spec, spec), out_specs=spec, check_vma=False
    )
```

```python
import functools

import jax
import jax.numpy as jnp
from jax import lax
from jax.experimental import pallas as pl
from jax.experimental.pallas import tpu as pltpu
from jax.sharding import PartitionSpec as P

C = 0.8 / 6.0
CS = 0.8 / 30.0
D1, D2, D3, D4 = C * 4.0, C * 16.0, C * 64.0, C * 256.0
MESH = pl.DeviceIdType.MESH
F32 = jnp.float32
BF16 = jnp.bfloat16


def roll(a, by, axis):
    return pltpu.roll(a, by % a.shape[axis], axis)


def pair_matrix(rows, cols, used_rows, used_cols, down):
    k = lax.broadcasted_iota(jnp.int32, (rows, cols), 0)
    j = lax.broadcasted_iota(jnp.int32, (rows, cols), 1)
    hit = (k // 2 == j) if down else (j // 2 == k)
    hit = hit & (k < used_rows) & (j < used_cols)
    return jnp.where(hit, 1.0, 0.0).astype(BF16)


def split_dot(x, matrix):
    hi = x.astype(BF16)
    rest = x - hi.astype(F32)
    mid = rest.astype(BF16)
    lo = (rest - mid.astype(F32)).astype(BF16)
    out = jnp.dot(hi, matrix, preferred_element_type=F32)
    out = out + jnp.dot(mid, matrix, preferred_element_type=F32)
    return out + jnp.dot(lo, matrix, preferred_element_type=F32)


def z_sum(a, full):
    left, right = roll(a, 1, 1), roll(a, -1, 1)
    if full:
        lane = lax.broadcasted_iota(jnp.int32, a.shape, 1)
        left = jnp.where(lane == 0, 0.0, left)
        right = jnp.where(lane == a.shape[1] - 1, 0.0, right)
    return left + right


def neighbors(a, planes, rows, full, mask_y=True):
    up, down = roll(a, 1, 0), roll(a, -1, 0)
    if mask_y:
        y = lax.broadcasted_iota(jnp.int32, a.shape, 0)
        y = y & (rows - 1) if rows & (rows - 1) == 0 else y % rows
        up = jnp.where(y == 0, 0.0, up)
        down = jnp.where(y == rows - 1, 0.0, down)
    zero = jnp.zeros((rows, a.shape[1]), F32)
    below = jnp.concatenate([zero, a[: (planes - 1) * rows]], 0)
    above = jnp.concatenate([a[rows:], zero], 0)
    return below + above + up + down + z_sum(a, full)


def x_pairs(a, planes, rows):
    return jnp.concatenate(
        [
            a[2 * i * rows : (2 * i + 1) * rows] + a[(2 * i + 1) * rows : (2 * i + 2) * rows]
            for i in range(planes // 2)
        ],
        0,
    )


def kernel(
    n, m, source_ref, obstacle_ref, out_ref,
    src, obs, xs, xr, y_out, y_in_ref, d_out, d_in, sf_ref, xh, yh, ys, r1, gathered, packed, a2, e3s, q2, e2s, e21, e1s, tmp,
    send, recv, gsend, grecv, load, ready,
):
    gx, gy = lax.axis_index("gx"), lax.axis_index("gy")
    windowed = n > 16
    window = 28 if windowed else 16
    yrows = 16 * m

    def base_of(x):
        return 4 * (x // 4) - 12 if windowed else 0

    base = base_of(gx)

    def peers(fn):
        if not windowed:
            flat = gx * m + gy
            for k in range(1, n * m):
                other = lax.rem(flat + k, n * m)
                fn(other // m, lax.rem(other, m))
            return

        def step(k, carry):
            x, y = base + k // m, lax.rem(k, m)

            @pl.when((x >= 0) & (x < n) & ((x != gx) | (y != gy)))
            def _():
                fn(x, y)

            return carry

        lax.fori_loop(0, window * m, step, 0)

    def exists(dx, dy):
        x, y = gx + dx, gy + dy
        return (x >= 0) & (x < n) & (y >= 0) & (y < m)

    def halo(k, src, dst, dx, dy):
        copy = pltpu.make_async_remote_copy(
            src_ref=src,
            dst_ref=dst,
            send_sem=send.at[k],
            recv_sem=recv.at[k],
            device_id=(jnp.clip(gx + dx, 0, n - 1), jnp.clip(gy + dy, 0, m - 1)),
            device_id_type=MESH,
        )

        def start():
            pl.when(exists(dx, dy))(lambda: copy.start())

        def wait_recv():
            pl.when(exists(-dx, -dy))(lambda: copy.wait_recv())

        def wait_send():
            pl.when(exists(dx, dy))(lambda: copy.wait_send())

        return start, wait_recv, wait_send

    loads = [
        pltpu.make_async_copy(source_ref, src, load.at[0]),
        pltpu.make_async_copy(obstacle_ref, obs, load.at[1]),
    ]
    for copy in loads:
        copy.start()
    xh[...] = jnp.zeros_like(xh)
    yh[...] = jnp.zeros_like(yh)
    r1[...] = jnp.zeros_like(r1)
    xr[...] = jnp.zeros_like(xr)
    y_in_ref[...] = jnp.zeros_like(y_in_ref)
    d_in[...] = jnp.zeros_like(d_in)
    if windowed:
        gathered[...] = jnp.zeros_like(gathered)
    barrier = pltpu.get_barrier_semaphore()

    def greet(x, y):
        pl.semaphore_signal(barrier, inc=1, device_id=(x, y), device_id_type=MESH)

    group = n * m // 4
    flat = gx * m + gy

    def counterparts(fn):
        for k in range(1, 4):
            other = lax.rem(flat + k * group, n * m)
            fn(other // m, lax.rem(other, m))

    def across(fn=None):
        count = 0
        for dx in (-1, 1):
            for dy in range(-1, 2):
                x, y = gx + dx, gy + dy
                fits = exists(dx, dy) & ((x * m + y) // group != flat // group)
                fits = fits & (lax.rem(x * m + y - flat + n * m, group) != 0)
                if fn is None:
                    count = count + jnp.where(fits, 1, 0)
                else:
                    pl.when(fits)(lambda x=x, y=y: fn(x, y))
        return count

    def first_stage(fn):
        if windowed:
            return peers(fn)
        for k in range(1, group):
            other = flat // group * group + lax.rem(flat + k, group)
            fn(other // m, lax.rem(other, m))
        counterparts(fn)
        across(fn)

    first_stage(greet)

    ys[...] = jnp.zeros_like(ys)
    y_out[...] = jnp.zeros_like(y_out)
    d_out[...] = jnp.zeros_like(d_out)
    e3s[...] = jnp.zeros_like(e3s)
    e2s[...] = jnp.zeros_like(e2s)
    a2[...] = jnp.zeros_like(a2)
    for copy in loads:
        copy.wait()
    for i in range(4):
        plane = jnp.where(obs[i] == 0, src[i], 0.0)
        sf_ref[i] = plane
        ys[0, i : i + 1, :] = plane[0:1]
        ys[1, i : i + 1, :] = plane[63:64]

    if windowed:
        total = 0
        for k in range(window * m):
            x, y = base + k // m, k % m
            total = total + jnp.where((x >= 0) & (x < n) & ((x != gx) | (y != gy)), 1, 0)
        pl.semaphore_wait(barrier, total)
    else:
        pl.semaphore_wait(barrier, group + 2 + across())
        counterparts(
            lambda x, y: pl.semaphore_signal(
                ready, inc=1, device_id=(x, y), device_id_type=MESH
            )
        )

    halos = []

    def add(src, dst, dx, dy):
        halos.append(halo(len(halos), src, dst, dx, dy))
        return halos[-1]

    zmat = pair_matrix(256, 128, 256, 128, True)
    row = lax.broadcasted_iota(jnp.int32, (64, 256), 0)
    row1 = lax.broadcasted_iota(jnp.int32, (32, 128), 0)

    def fine_neighbors(planes, i, above_row, below_row):
        p = planes[i + 1]
        up = jnp.where(row == 0, above_row, roll(p, 1, 0))
        down = jnp.where(row == 63, below_row, roll(p, -1, 0))
        return planes[i] + planes[i + 2] + up + down + z_sum(p, True)

    zero = jnp.zeros((64, 256), F32)
    fine = [sf_ref[i] for i in range(4)]
    padded = [zero] + fine + [zero]
    left = [0.2 * fine[i] + C * fine_neighbors(padded, i, 0.0, 0.0) for i in range(4)]
    rim = [C * (fine[2 * i][r : r + 1] + fine[2 * i + 1][r : r + 1]) for i in (0, 1) for r in (0, 63)]
    rows_in = [left[0] + left[1], left[2] + left[3], C * fine[0], C * fine[3]]
    rows_in += rim + [jnp.zeros((4, 256), F32)]
    tmp[0:264] = split_dot(jnp.concatenate(rows_in, 0), zmat) * 0.125
    part0, part1, side0, side1 = [
        tmp[pl.ds(64 * i, 32, stride=2), :] + tmp[pl.ds(64 * i + 1, 32, stride=2), :]
        for i in range(4)
    ]
    edge = [[tmp[256 + 2 * i + r : 257 + 2 * i + r, :] for r in (0, 1)] for i in (0, 1)]
    parts, sides = (part0, part1), (side0, side1)
    for i in (0, 1):
        xs[i, 0] = parts[i]
        xs[i, 1] = sides[i]
    for r in (0, 1):
        cut = slice(31 * r, 31 * r + 1)
        for i in (0, 1):
            y_out[r, i : i + 1, :] = parts[i][cut]
            y_out[r, 2 + i : 3 + i, :] = edge[i][r]
            d_out[2 * i + r, 0:1, :] = edge[i][r]
            d_out[2 * i + r, 1:2, :] = sides[i][cut]
    first = [
        add(xs.at[1], xr.at[0], 1, 0),
        add(xs.at[0], xr.at[1], -1, 0),
        add(y_out.at[1], y_in_ref.at[0], 0, 1),
        add(y_out.at[0], y_in_ref.at[1], 0, -1),
        add(d_out.at[3], d_in.at[0], 1, 1),
        add(d_out.at[2], d_in.at[1], 1, -1),
        add(d_out.at[1], d_in.at[2], -1, 1),
        add(d_out.at[0], d_in.at[3], -1, -1),
    ]
    for start, _, _ in first:
        start()
    for _, wait, _ in first:
        wait()

    def with_edges(a, top, bottom):
        a = a + jnp.where(row1 == 0, top, 0.0)
        return a + jnp.where(row1 == 31, bottom, 0.0)

    alive = [jnp.where(gx > 0, 1.0, 0.0), 1.0, jnp.where(gx < n - 1, 1.0, 0.0)]
    own = []
    for i in (0, 1):
        a = parts[i] + xr[i, 1]
        own.append(with_edges(a, y_in_ref[0, 2 + i : 3 + i, :], y_in_ref[1, 2 + i : 3 + i, :]))
    beside = []
    for i in (0, 1):
        a = xr[i, 0] + sides[i]
        a = with_edges(a, d_in[2 * i, 0:1, :], d_in[2 * i + 1, 0:1, :])
        beside.append(a * alive[2 * i])
    y_alive = [jnp.where(gy > 0, 1.0, 0.0), jnp.where(gy < m - 1, 1.0, 0.0)]
    rim1 = [
        [
            y_alive[r] * (y_in_ref[r, i : i + 1, :] + edge[i][r] + d_in[2 * i + r, 1:2, :])
            for r in (0, 1)
        ]
        for i in (0, 1)
    ]
    left1 = []
    for i in (0, 1):
        p = own[i]
        up = jnp.where(row1 == 0, rim1[i][0], roll(p, 1, 0))
        down = jnp.where(row1 == 31, rim1[i][1], roll(p, -1, 0))
        total = beside[i] + own[1 - i] + up + down + z_sum(p, True)
        left1.append(0.2 * p + C * total)
    tmp[0:32] = split_dot(left1[0] + left1[1], pair_matrix(128, 128, 128, 64, True)) * 0.125
    r2 = tmp[pl.ds(0, 16, stride=2), :] + tmp[pl.ds(1, 16, stride=2), :]
    mine = r2[0:8] + roll(r2[8:16], 64, 1)
    packed[...] = mine
    gathered[(gx - base) * m + gy] = mine

    def tile_copy(x, y):
        return pltpu.make_async_remote_copy(
            src_ref=packed,
            dst_ref=gathered.at[(gx - base_of(x)) * m + gy],
            send_sem=gsend,
            recv_sem=grecv,
            device_id=(x, y),
            device_id_type=MESH,
        )

    if not windowed:
        pl.semaphore_wait(ready, 3)
    peers(lambda x, y: tile_copy(x, y).start())
    for i in (0, 1):
        r1[2 + i, 8:40, :] = own[i]
        r1[1 + 3 * i, 8:40, :] = beside[i]
    mid = pl.ds(8, 32)
    third = [
        add(r1.at[2, mid], r1.at[0, mid], 1, 0),
        add(r1.at[3, mid], r1.at[5, mid], -1, 0),
        add(r1.at[pl.ds(2, 2), pl.ds(32, 8)], r1.at[pl.ds(2, 2), pl.ds(0, 8)], 0, 1),
        add(r1.at[pl.ds(2, 2), pl.ds(8, 8)], r1.at[pl.ds(2, 2), pl.ds(40, 8)], 0, -1),
        add(r1.at[3, pl.ds(32, 8)], r1.at[1, pl.ds(0, 8)], 1, 1),
        add(r1.at[3, pl.ds(8, 8)], r1.at[1, pl.ds(40, 8)], 1, -1),
        add(r1.at[2, pl.ds(32, 8)], r1.at[4, pl.ds(0, 8)], -1, 1),
        add(r1.at[2, pl.ds(8, 8)], r1.at[4, pl.ds(40, 8)], -1, -1),
        add(sf_ref.at[3], xh.at[0], 1, 0),
        add(sf_ref.at[0], xh.at[1], -1, 0),
        add(ys.at[1], yh.at[0], 0, 1),
        add(ys.at[0], yh.at[1], 0, -1),
    ]
    for start, _, _ in third:
        start()
    if not windowed:
        many = gathered.at[pl.ds(0, n * m - 1)]
        pltpu.make_async_copy(many, many, grecv).wait()
    else:
        peers(lambda x, y: tile_copy(x, y).wait_recv())

    def inside(a, planes, rows, first_plane, count):
        if not windowed:
            return a
        x = first_plane + lax.broadcasted_iota(jnp.int32, a.shape, 0) // rows
        return jnp.where((x >= 0) & (x < count), a, 0.0)

    tiles = gathered[...].reshape(window * m * 8, 128)
    lane = lax.broadcasted_iota(jnp.int32, tiles.shape, 1)
    low = jnp.where(lane < 64, tiles, 0.0).reshape(window * m, 8, 128)
    high = jnp.where(lane < 64, roll(tiles, 64, 1), 0.0).reshape(window * m, 8, 128)
    a2[pl.ds(2 * m, window * m), 0:8, :] = low
    a2[pl.ds(2 * m, window * m), 8:16, :] = high
    full2 = a2[pl.ds(2 * m, window * m)].reshape(window * yrows, 128)

    def restrict(a, planes, rows, used):
        count = planes // 2 * rows
        folded = x_pairs(a, planes, rows)
        tmp[0:count] = split_dot(folded, pair_matrix(128, 128, used, used // 2, True)) * 0.125
        half = count // 2
        return tmp[pl.ds(0, half, stride=2), :] + tmp[pl.ds(1, half, stride=2), :]

    def prolong_yz(a, used, dst):
        wide = split_dot(a, pair_matrix(128, 128, used, used * 2, False))
        dst[pl.ds(0, a.shape[0], stride=2), :] = wide
        dst[pl.ds(1, a.shape[0], stride=2), :] = wide

    x3, y3 = window // 2, yrows // 2
    x4, y4 = window // 4, yrows // 4
    r3 = restrict(0.2 * full2 + C * neighbors(full2, window, yrows, False), window, yrows, 64)
    r4 = restrict(0.2 * r3 + C * neighbors(r3, x3, y3, False), x3, y3, 32)
    e4 = D4 * (1.2 * r4 + C * neighbors(r4, x4, y4, False))
    e4 = inside(e4, x4, y4, base // 4, n // 4)
    prolong_yz(e4, 16, tmp)
    e3 = D3 * r3 + jnp.concatenate(
        [tmp[pl.ds((i // 2) * y3, y3), :] for i in range(x3)], 0
    )
    e3 = 0.2 * e3 + D3 * r3 + C * neighbors(e3, x3, y3, False)
    e3 = inside(e3, x3, y3, base // 2, n // 2)
    e3s[pl.ds(1, x3)] = e3.reshape(x3, y3, 128)

    low3 = (gx - base + 2) // 2 - 1
    prolong_yz(e3s[pl.ds(low3, 3)].reshape(3 * y3, 128), 32, q2)
    odd = lax.rem(gx, 2)
    rs, es = [], []
    for d in range(-2, 3):
        plane = a2[pl.ds((gx - base + 2 + d) * m, m)].reshape(yrows, 128)
        start = pl.multiple_of(((odd + d + 2) // 2) * yrows, 8)
        rs.append(plane)
        es.append(D2 * plane + q2[pl.ds(start, yrows), :])
    rs, es = jnp.concatenate(rs, 0), jnp.concatenate(es, 0)
    e2 = 0.2 * es + D2 * rs + C * neighbors(es, 5, yrows, False)
    e2 = e2[yrows : 4 * yrows]
    wide = split_dot(e2, pair_matrix(128, 128, 64, 128, False))
    for i in range(3):
        e2s[i, pl.ds(8, yrows), :] = wide[i * yrows : (i + 1) * yrows] * alive[i]
    for i in range(3):
        part = e2s[i, pl.ds(gy * 16 + 4, 24), :]
        e21[pl.ds(48 * i, 24, stride=2), :] = part
        e21[pl.ds(48 * i + 1, 24, stride=2), :] = part

    for _, wait, _ in third:
        wait()
    r1s = [r1[k] for k in range(6)]
    e1p = [D1 * r1s[k] + e21[48 * (k // 2) : 48 * (k // 2) + 48, :] for k in range(6)]
    y = gy * 32 - 8 + lax.broadcasted_iota(jnp.int32, (48, 128), 0)
    y_in = (y >= 0) & (y < 32 * m)
    done = []
    for k in range(1, 5):
        p = e1p[k]
        total = e1p[k - 1] + e1p[k + 1] + roll(p, 1, 0) + roll(p, -1, 0) + z_sum(p, True)
        value = jnp.where(y_in, 0.2 * p + D1 * r1s[k] + C * total, 0.0)
        if k == 1:
            value = value * alive[0]
        if k == 4:
            value = value * alive[2]
        done.append(value)
    done = jnp.concatenate(done, 0)
    wide = split_dot(done, pair_matrix(128, 256, 128, 256, False))
    for h in range(2):
        half = wide[:, 128 * h : 128 * h + 128]
        e1s[h, pl.ds(0, 192, stride=2), :] = half
        e1s[h, pl.ds(1, 192, stride=2), :] = half

    def coarse(k, start, rows):
        return jnp.concatenate([e1s[h, 96 * k + start : 96 * k + start + rows, :] for h in (0, 1)], 1)

    blocks = [coarse(k, 16, 64) for k in range(4)]
    planes = [C * xh[0] + blocks[0]]
    planes += [C * sf_ref[i] + blocks[1 + i // 2] for i in range(4)]
    planes += [C * xh[1] + blocks[3]]
    for i in range(4):
        k = 1 + i // 2
        above = C * yh[0, i : i + 1, :] + coarse(k, 15, 1)
        below = C * yh[1, i : i + 1, :] + coarse(k, 80, 1)
        total = fine_neighbors(planes, i, above, below)
        weight = jnp.where(obs[i] == 0, C, CS)
        out_ref[i] = 0.2 * planes[i + 1] + weight * (sf_ref[i] + total)

    for _, _, wait in halos:
        wait()
    if not windowed:
        many = gathered.at[pl.ds(0, n * m - 1)]
        pltpu.make_async_copy(many, many, gsend).wait()
    else:
        peers(lambda x, y: tile_copy(x, y).wait_send())


def solution(mesh):
    n, m = mesh.shape["gx"], mesh.shape["gy"]
    window = 28 if n > 16 else 16
    rows = 16 * m

    def body(source, obstacle):
        vmem = pl.BlockSpec(memory_space=pltpu.VMEM)
        return pl.pallas_call(
            functools.partial(kernel, n, m),
            out_shape=jax.ShapeDtypeStruct(source.shape, F32),
            in_specs=[pl.BlockSpec(memory_space=pltpu.HBM)] * 2,
            out_specs=vmem,
            scratch_shapes=[
                pltpu.VMEM(source.shape, F32),
                pltpu.VMEM(source.shape, jnp.int32),
                pltpu.VMEM((2, 2, 32, 128), F32),
                pltpu.VMEM((2, 2, 32, 128), F32),
                pltpu.VMEM((2, 8, 128), F32),
                pltpu.VMEM((2, 8, 128), F32),
                pltpu.VMEM((4, 8, 128), F32),
                pltpu.VMEM((4, 8, 128), F32),
                pltpu.VMEM((4, 64, 256), F32),
                pltpu.VMEM((2, 64, 256), F32),
                pltpu.VMEM((2, 8, 256), F32),
                pltpu.VMEM((2, 8, 256), F32),
                pltpu.VMEM((6, 48, 128), F32),
                pltpu.VMEM((window * m, 8, 128), F32),
                pltpu.VMEM((8, 128), F32),
                pltpu.VMEM(((window + 4) * m, 16, 128), F32),
                pltpu.VMEM((window // 2 + 2, rows // 2, 128), F32),
                pltpu.VMEM((3 * rows, 128), F32),
                pltpu.VMEM((3, rows + 16, 128), F32),
                pltpu.VMEM((144, 128), F32),
                pltpu.VMEM((2, 384, 128), F32),
                pltpu.VMEM((max(264, window // 2 * rows), 128), F32),
                pltpu.SemaphoreType.DMA((20,)),
                pltpu.SemaphoreType.DMA((20,)),
                pltpu.SemaphoreType.DMA,
                pltpu.SemaphoreType.DMA,
                pltpu.SemaphoreType.DMA((2,)),
                pltpu.SemaphoreType.REGULAR,
            ],
            compiler_params=pltpu.CompilerParams(
                collective_id=0, has_side_effects=True, vmem_limit_bytes=32 * 1024 * 1024
            ),
        )(source, obstacle)

    spec = P("gx", "gy", None)
    return jax.shard_map(
        body, mesh=mesh, in_specs=(spec, spec), out_specs=spec, check_vma=False
    )
```

```python
import functools

import jax
import jax.numpy as jnp
from jax import lax
from jax.experimental import pallas as pl
from jax.experimental.pallas import tpu as pltpu
from jax.sharding import PartitionSpec as P

C = 0.8 / 6.0
CS = 0.8 / 30.0
D1, D2, D3, D4 = C * 4.0, C * 16.0, C * 64.0, C * 256.0
MESH = pl.DeviceIdType.MESH
F32 = jnp.float32
BF16 = jnp.bfloat16


def roll(a, by, axis):
    return pltpu.roll(a, by % a.shape[axis], axis)


def pair_matrix(rows, cols, used_rows, used_cols, down):
    k = lax.broadcasted_iota(jnp.int32, (rows, cols), 0)
    j = lax.broadcasted_iota(jnp.int32, (rows, cols), 1)
    hit = (k // 2 == j) if down else (j // 2 == k)
    hit = hit & (k < used_rows) & (j < used_cols)
    return jnp.where(hit, 1.0, 0.0).astype(BF16)


def split_dot(x, matrix):
    hi = x.astype(BF16)
    rest = x - hi.astype(F32)
    mid = rest.astype(BF16)
    lo = (rest - mid.astype(F32)).astype(BF16)
    out = jnp.dot(hi, matrix, preferred_element_type=F32)
    out = out + jnp.dot(mid, matrix, preferred_element_type=F32)
    return out + jnp.dot(lo, matrix, preferred_element_type=F32)


def z_sum(a, full):
    left, right = roll(a, 1, 1), roll(a, -1, 1)
    if full:
        lane = lax.broadcasted_iota(jnp.int32, a.shape, 1)
        left = jnp.where(lane == 0, 0.0, left)
        right = jnp.where(lane == a.shape[1] - 1, 0.0, right)
    return left + right


def neighbors(a, planes, rows, full, mask_y=True):
    up, down = roll(a, 1, 0), roll(a, -1, 0)
    if mask_y:
        y = lax.broadcasted_iota(jnp.int32, a.shape, 0)
        y = y & (rows - 1) if rows & (rows - 1) == 0 else y % rows
        up = jnp.where(y == 0, 0.0, up)
        down = jnp.where(y == rows - 1, 0.0, down)
    zero = jnp.zeros((rows, a.shape[1]), F32)
    below = jnp.concatenate([zero, a[: (planes - 1) * rows]], 0)
    above = jnp.concatenate([a[rows:], zero], 0)
    return below + above + up + down + z_sum(a, full)


def x_pairs(a, planes, rows):
    return jnp.concatenate(
        [
            a[2 * i * rows : (2 * i + 1) * rows] + a[(2 * i + 1) * rows : (2 * i + 2) * rows]
            for i in range(planes // 2)
        ],
        0,
    )


def kernel(
    n, m, source_ref, obstacle_ref, out_ref,
    src, obs, xs, xr, y_out, y_in_ref, d_out, d_in, sf_ref, xh, yh, ys, r1, gathered, packed, a2, e3s, q2, e2s, e21, e1s, tmp,
    send, recv, gsend, grecv, load, ready,
):
    gx, gy = lax.axis_index("gx"), lax.axis_index("gy")
    windowed = n > 16
    window = 28 if windowed else 16
    yrows = 16 * m

    def base_of(x):
        return 4 * (x // 4) - 12 if windowed else 0

    base = base_of(gx)

    def peers(fn):
        if not windowed:
            flat = gx * m + gy
            for k in range(1, n * m):
                other = lax.rem(flat + k, n * m)
                fn(other // m, lax.rem(other, m))
            return

        def step(k, carry):
            x, y = base + k // m, lax.rem(k, m)

            @pl.when((x >= 0) & (x < n) & ((x != gx) | (y != gy)))
            def _():
                fn(x, y)

            return carry

        lax.fori_loop(0, window * m, step, 0)

    def exists(dx, dy):
        x, y = gx + dx, gy + dy
        return (x >= 0) & (x < n) & (y >= 0) & (y < m)

    def halo(k, src, dst, dx, dy):
        copy = pltpu.make_async_remote_copy(
            src_ref=src,
            dst_ref=dst,
            send_sem=send.at[k],
            recv_sem=recv.at[k],
            device_id=(jnp.clip(gx + dx, 0, n - 1), jnp.clip(gy + dy, 0, m - 1)),
            device_id_type=MESH,
        )

        def start():
            pl.when(exists(dx, dy))(lambda: copy.start())

        def wait_recv():
            pl.when(exists(-dx, -dy))(lambda: copy.wait_recv())

        def wait_send():
            pl.when(exists(dx, dy))(lambda: copy.wait_send())

        return start, wait_recv, wait_send

    loads = [
        pltpu.make_async_copy(source_ref, src, load.at[0]),
        pltpu.make_async_copy(obstacle_ref, obs, load.at[1]),
    ]
    for copy in loads:
        copy.start()
    xh[...] = jnp.zeros_like(xh)
    yh[...] = jnp.zeros_like(yh)
    r1[...] = jnp.zeros_like(r1)
    xr[...] = jnp.zeros_like(xr)
    y_in_ref[...] = jnp.zeros_like(y_in_ref)
    d_in[...] = jnp.zeros_like(d_in)
    if windowed:
        gathered[...] = jnp.zeros_like(gathered)
    barrier = pltpu.get_barrier_semaphore()

    def greet(x, y):
        pl.semaphore_signal(barrier, inc=1, device_id=(x, y), device_id_type=MESH)

    group = n * m // 4
    flat = gx * m + gy

    def counterparts(fn):
        for k in range(1, 4):
            other = lax.rem(flat + k * group, n * m)
            fn(other // m, lax.rem(other, m))

    def across(fn=None):
        count = 0
        for dx in (-1, 1):
            for dy in range(-1, 2):
                x, y = gx + dx, gy + dy
                fits = exists(dx, dy) & ((x * m + y) // group != flat // group)
                fits = fits & (lax.rem(x * m + y - flat + n * m, group) != 0)
                if fn is None:
                    count = count + jnp.where(fits, 1, 0)
                else:
                    pl.when(fits)(lambda x=x, y=y: fn(x, y))
        return count

    def first_stage(fn):
        if windowed:
            return peers(fn)
        for k in range(1, group):
            other = flat // group * group + lax.rem(flat + k, group)
            fn(other // m, lax.rem(other, m))
        counterparts(fn)
        across(fn)

    first_stage(greet)

    ys[...] = jnp.zeros_like(ys)
    y_out[...] = jnp.zeros_like(y_out)
    d_out[...] = jnp.zeros_like(d_out)
    e3s[...] = jnp.zeros_like(e3s)
    e2s[...] = jnp.zeros_like(e2s)
    a2[...] = jnp.zeros_like(a2)
    for copy in loads:
        copy.wait()
    for i in range(4):
        plane = jnp.where(obs[i] == 0, src[i], 0.0)
        sf_ref[i] = plane
        ys[0, i : i + 1, :] = plane[0:1]
        ys[1, i : i + 1, :] = plane[63:64]

    if windowed:
        total = 0
        for k in range(window * m):
            x, y = base + k // m, k % m
            total = total + jnp.where((x >= 0) & (x < n) & ((x != gx) | (y != gy)), 1, 0)
        pl.semaphore_wait(barrier, total)
    else:
        pl.semaphore_wait(barrier, group + 2 + across())
        counterparts(
            lambda x, y: pl.semaphore_signal(
                ready, inc=1, device_id=(x, y), device_id_type=MESH
            )
        )

    halos = []

    def add(src, dst, dx, dy):
        halos.append(halo(len(halos), src, dst, dx, dy))
        return halos[-1]

    zmat = pair_matrix(256, 128, 256, 128, True)
    row = lax.broadcasted_iota(jnp.int32, (64, 256), 0)
    row1 = lax.broadcasted_iota(jnp.int32, (32, 128), 0)

    def fine_neighbors(planes, i, above_row, below_row):
        p = planes[i + 1]
        up = jnp.where(row == 0, above_row, roll(p, 1, 0))
        down = jnp.where(row == 63, below_row, roll(p, -1, 0))
        return planes[i] + planes[i + 2] + up + down + z_sum(p, True)

    zero = jnp.zeros((64, 256), F32)
    fine = [sf_ref[i] for i in range(4)]
    padded = [zero] + fine + [zero]
    left = [0.2 * fine[i] + C * fine_neighbors(padded, i, 0.0, 0.0) for i in range(4)]
    rim = [C * (fine[2 * i][r : r + 1] + fine[2 * i + 1][r : r + 1]) for i in (0, 1) for r in (0, 63)]
    rows_in = [left[0] + left[1], left[2] + left[3], C * fine[0], C * fine[3]]
    rows_in += rim + [jnp.zeros((4, 256), F32)]
    tmp[0:264] = split_dot(jnp.concatenate(rows_in, 0), zmat) * 0.125
    part0, part1, side0, side1 = [
        tmp[pl.ds(64 * i, 32, stride=2), :] + tmp[pl.ds(64 * i + 1, 32, stride=2), :]
        for i in range(4)
    ]
    edge = [[tmp[256 + 2 * i + r : 257 + 2 * i + r, :] for r in (0, 1)] for i in (0, 1)]
    parts, sides = (part0, part1), (side0, side1)
    for i in (0, 1):
        xs[i, 0] = parts[i]
        xs[i, 1] = sides[i]
    for r in (0, 1):
        cut = slice(31 * r, 31 * r + 1)
        for i in (0, 1):
            y_out[r, i : i + 1, :] = parts[i][cut]
            y_out[r, 2 + i : 3 + i, :] = edge[i][r]
            d_out[2 * i + r, 0:1, :] = edge[i][r]
            d_out[2 * i + r, 1:2, :] = sides[i][cut]
    first = [
        add(xs.at[1], xr.at[0], 1, 0),
        add(xs.at[0], xr.at[1], -1, 0),
        add(y_out.at[1], y_in_ref.at[0], 0, 1),
        add(y_out.at[0], y_in_ref.at[1], 0, -1),
        add(d_out.at[3], d_in.at[0], 1, 1),
        add(d_out.at[2], d_in.at[1], 1, -1),
        add(d_out.at[1], d_in.at[2], -1, 1),
        add(d_out.at[0], d_in.at[3], -1, -1),
    ]
    for start, _, _ in first:
        start()
    for _, wait, _ in first:
        wait()

    def with_edges(a, top, bottom):
        a = a + jnp.where(row1 == 0, top, 0.0)
        return a + jnp.where(row1 == 31, bottom, 0.0)

    alive = [jnp.where(gx > 0, 1.0, 0.0), 1.0, jnp.where(gx < n - 1, 1.0, 0.0)]
    own = []
    for i in (0, 1):
        a = parts[i] + xr[i, 1]
        own.append(with_edges(a, y_in_ref[0, 2 + i : 3 + i, :], y_in_ref[1, 2 + i : 3 + i, :]))
    beside = []
    for i in (0, 1):
        a = xr[i, 0] + sides[i]
        a = with_edges(a, d_in[2 * i, 0:1, :], d_in[2 * i + 1, 0:1, :])
        beside.append(a * alive[2 * i])
    y_alive = [jnp.where(gy > 0, 1.0, 0.0), jnp.where(gy < m - 1, 1.0, 0.0)]
    rim1 = [
        [
            y_alive[r] * (y_in_ref[r, i : i + 1, :] + edge[i][r] + d_in[2 * i + r, 1:2, :])
            for r in (0, 1)
        ]
        for i in (0, 1)
    ]
    left1 = []
    for i in (0, 1):
        p = own[i]
        up = jnp.where(row1 == 0, rim1[i][0], roll(p, 1, 0))
        down = jnp.where(row1 == 31, rim1[i][1], roll(p, -1, 0))
        total = beside[i] + own[1 - i] + up + down + z_sum(p, True)
        left1.append(0.2 * p + C * total)
    tmp[0:32] = split_dot(left1[0] + left1[1], pair_matrix(128, 128, 128, 64, True)) * 0.125
    r2 = tmp[pl.ds(0, 16, stride=2), :] + tmp[pl.ds(1, 16, stride=2), :]
    mine = r2[0:8] + roll(r2[8:16], 64, 1)
    packed[...] = mine
    gathered[(gx - base) * m + gy] = mine

    def tile_copy(x, y):
        return pltpu.make_async_remote_copy(
            src_ref=packed,
            dst_ref=gathered.at[(gx - base_of(x)) * m + gy],
            send_sem=gsend,
            recv_sem=grecv,
            device_id=(x, y),
            device_id_type=MESH,
        )

    if not windowed:
        pl.semaphore_wait(ready, 3)
    peers(lambda x, y: tile_copy(x, y).start())
    for i in (0, 1):
        r1[2 + i, 8:40, :] = own[i]
        r1[1 + 3 * i, 8:40, :] = beside[i]
    mid = pl.ds(8, 32)
    third = [
        add(r1.at[2, mid], r1.at[0, mid], 1, 0),
        add(r1.at[3, mid], r1.at[5, mid], -1, 0),
        add(r1.at[pl.ds(2, 2), pl.ds(32, 8)], r1.at[pl.ds(2, 2), pl.ds(0, 8)], 0, 1),
        add(r1.at[pl.ds(2, 2), pl.ds(8, 8)], r1.at[pl.ds(2, 2), pl.ds(40, 8)], 0, -1),
        add(r1.at[3, pl.ds(32, 8)], r1.at[1, pl.ds(0, 8)], 1, 1),
        add(r1.at[3, pl.ds(8, 8)], r1.at[1, pl.ds(40, 8)], 1, -1),
        add(r1.at[2, pl.ds(32, 8)], r1.at[4, pl.ds(0, 8)], -1, 1),
        add(r1.at[2, pl.ds(8, 8)], r1.at[4, pl.ds(40, 8)], -1, -1),
        add(sf_ref.at[3], xh.at[0], 1, 0),
        add(sf_ref.at[0], xh.at[1], -1, 0),
        add(ys.at[1], yh.at[0], 0, 1),
        add(ys.at[0], yh.at[1], 0, -1),
    ]
    for start, _, _ in third:
        start()
    if not windowed:
        many = gathered.at[pl.ds(0, n * m - 1)]
        pltpu.make_async_copy(many, many, grecv).wait()
    else:
        peers(lambda x, y: tile_copy(x, y).wait_recv())

    def inside(a, planes, rows, first_plane, count):
        if not windowed:
            return a
        x = first_plane + lax.broadcasted_iota(jnp.int32, a.shape, 0) // rows
        return jnp.where((x >= 0) & (x < count), a, 0.0)

    tiles = gathered[...].reshape(window * m * 8, 128)
    lane = lax.broadcasted_iota(jnp.int32, tiles.shape, 1)
    low = jnp.where(lane < 64, tiles, 0.0).reshape(window * m, 8, 128)
    high = jnp.where(lane < 64, roll(tiles, 64, 1), 0.0).reshape(window * m, 8, 128)
    a2[pl.ds(2 * m, window * m), 0:8, :] = low
    a2[pl.ds(2 * m, window * m), 8:16, :] = high
    full2 = a2[pl.ds(2 * m, window * m)].reshape(window * yrows, 128)

    def restrict(a, planes, rows, used):
        count = planes // 2 * rows
        folded = x_pairs(a, planes, rows)
        tmp[0:count] = split_dot(folded, pair_matrix(128, 128, used, used // 2, True)) * 0.125
        half = count // 2
        return tmp[pl.ds(0, half, stride=2), :] + tmp[pl.ds(1, half, stride=2), :]

    def prolong_yz(a, used, dst):
        wide = split_dot(a, pair_matrix(128, 128, used, used * 2, False))
        dst[pl.ds(0, a.shape[0], stride=2), :] = wide
        dst[pl.ds(1, a.shape[0], stride=2), :] = wide

    x3, y3 = window // 2, yrows // 2
    x4, y4 = window // 4, yrows // 4
    r3 = restrict(0.2 * full2 + C * neighbors(full2, window, yrows, False), window, yrows, 64)
    r4 = restrict(0.2 * r3 + C * neighbors(r3, x3, y3, False), x3, y3, 32)
    e4 = D4 * (1.2 * r4 + C * neighbors(r4, x4, y4, False))
    e4 = inside(e4, x4, y4, base // 4, n // 4)
    prolong_yz(e4, 16, tmp)
    e3 = D3 * r3 + jnp.concatenate(
        [tmp[pl.ds((i // 2) * y3, y3), :] for i in range(x3)], 0
    )
    e3 = 0.2 * e3 + D3 * r3 + C * neighbors(e3, x3, y3, False)
    e3 = inside(e3, x3, y3, base // 2, n // 2)
    e3s[pl.ds(1, x3)] = e3.reshape(x3, y3, 128)

    low3 = (gx - base + 2) // 2 - 1
    prolong_yz(e3s[pl.ds(low3, 3)].reshape(3 * y3, 128), 32, q2)
    odd = lax.rem(gx, 2)
    rs, es = [], []
    for d in range(-2, 3):
        plane = a2[pl.ds((gx - base + 2 + d) * m, m)].reshape(yrows, 128)
        start = pl.multiple_of(((odd + d + 2) // 2) * yrows, 8)
        rs.append(plane)
        es.append(D2 * plane + q2[pl.ds(start, yrows), :])
    rs, es = jnp.concatenate(rs, 0), jnp.concatenate(es, 0)
    e2 = 0.2 * es + D2 * rs + C * neighbors(es, 5, yrows, False)
    e2 = e2[yrows : 4 * yrows]
    wide = split_dot(e2, pair_matrix(128, 128, 64, 128, False))
    for i in range(3):
        e2s[i, pl.ds(8, yrows), :] = wide[i * yrows : (i + 1) * yrows] * alive[i]
    for i in range(3):
        part = e2s[i, pl.ds(gy * 16 + 4, 24), :]
        e21[pl.ds(48 * i, 24, stride=2), :] = part
        e21[pl.ds(48 * i + 1, 24, stride=2), :] = part

    for _, wait, _ in third:
        wait()
    r1s = [r1[k] for k in range(6)]
    e1p = [D1 * r1s[k] + e21[48 * (k // 2) : 48 * (k // 2) + 48, :] for k in range(6)]
    y = gy * 32 - 8 + lax.broadcasted_iota(jnp.int32, (48, 128), 0)
    y_in = (y >= 0) & (y < 32 * m)
    done = []
    for k in range(1, 5):
        p = e1p[k]
        total = e1p[k - 1] + e1p[k + 1] + roll(p, 1, 0) + roll(p, -1, 0) + z_sum(p, True)
        value = jnp.where(y_in, 0.2 * p + D1 * r1s[k] + C * total, 0.0)
        if k == 1:
            value = value * alive[0]
        if k == 4:
            value = value * alive[2]
        done.append(value)
    done = jnp.concatenate(done, 0)
    wide = split_dot(done, pair_matrix(128, 256, 128, 256, False))
    for h in range(2):
        half = wide[:, 128 * h : 128 * h + 128]
        e1s[h, pl.ds(0, 192, stride=2), :] = half
        e1s[h, pl.ds(1, 192, stride=2), :] = half

    def coarse(k, start, rows):
        return jnp.concatenate([e1s[h, 96 * k + start : 96 * k + start + rows, :] for h in (0, 1)], 1)

    blocks = [coarse(k, 16, 64) for k in range(4)]
    planes = [C * xh[0] + blocks[0]]
    planes += [C * sf_ref[i] + blocks[1 + i // 2] for i in range(4)]
    planes += [C * xh[1] + blocks[3]]
    for i in range(4):
        k = 1 + i // 2
        above = C * yh[0, i : i + 1, :] + coarse(k, 15, 1)
        below = C * yh[1, i : i + 1, :] + coarse(k, 80, 1)
        total = fine_neighbors(planes, i, above, below)
        weight = jnp.where(obs[i] == 0, C, CS)
        out_ref[i] = 0.2 * planes[i + 1] + weight * (sf_ref[i] + total)

    for _, _, wait in halos:
        wait()
    if not windowed:
        many = gathered.at[pl.ds(0, n * m - 1)]
        pltpu.make_async_copy(many, many, gsend).wait()
    else:
        peers(lambda x, y: tile_copy(x, y).wait_send())


def solution(mesh):
    n, m = mesh.shape["gx"], mesh.shape["gy"]
    window = 28 if n > 16 else 16
    rows = 16 * m

    def body(source, obstacle):
        vmem = pl.BlockSpec(memory_space=pltpu.VMEM)
        return pl.pallas_call(
            functools.partial(kernel, n, m),
            out_shape=pltpu.VMEM(source.shape, F32),
            in_specs=[pl.BlockSpec(memory_space=pltpu.HBM)] * 2,
            out_specs=vmem,
            scratch_shapes=[
                pltpu.VMEM(source.shape, F32),
                pltpu.VMEM(source.shape, jnp.int32),
                pltpu.VMEM((2, 2, 32, 128), F32),
                pltpu.VMEM((2, 2, 32, 128), F32),
                pltpu.VMEM((2, 8, 128), F32),
                pltpu.VMEM((2, 8, 128), F32),
                pltpu.VMEM((4, 8, 128), F32),
                pltpu.VMEM((4, 8, 128), F32),
                pltpu.VMEM((4, 64, 256), F32),
                pltpu.VMEM((2, 64, 256), F32),
                pltpu.VMEM((2, 8, 256), F32),
                pltpu.VMEM((2, 8, 256), F32),
                pltpu.VMEM((6, 48, 128), F32),
                pltpu.VMEM((window * m, 8, 128), F32),
                pltpu.VMEM((8, 128), F32),
                pltpu.VMEM(((window + 4) * m, 16, 128), F32),
                pltpu.VMEM((window // 2 + 2, rows // 2, 128), F32),
                pltpu.VMEM((3 * rows, 128), F32),
                pltpu.VMEM((3, rows + 16, 128), F32),
                pltpu.VMEM((144, 128), F32),
                pltpu.VMEM((2, 384, 128), F32),
                pltpu.VMEM((max(264, window // 2 * rows), 128), F32),
                pltpu.SemaphoreType.DMA((20,)),
                pltpu.SemaphoreType.DMA((20,)),
                pltpu.SemaphoreType.DMA,
                pltpu.SemaphoreType.DMA,
                pltpu.SemaphoreType.DMA((2,)),
                pltpu.SemaphoreType.REGULAR,
            ],
            compiler_params=pltpu.CompilerParams(
                collective_id=0, has_side_effects=True, vmem_limit_bytes=56 * 1024 * 1024
            ),
        )(source, obstacle)

    spec = P("gx", "gy", None)
    return jax.shard_map(
        body, mesh=mesh, in_specs=(spec, spec), out_specs=spec, check_vma=False
    )
```
